1024 devices in a mesh: row: 16 (over x, z_hi, core), col: 64 (over z_lo, y).
Axes of the slice: x: 4, y: 4, z: 32 (z_hi: 2, z_lo: 16; z = z_hi * 16 + z_lo), core: 2. Of those that a mesh axis runs over, the one named last changes fastest.
Arguments:
- x_blocks: bfloat16 [3072, 128, 128], P(('row', 'col')), may hold values from -2 to 2
- x_cols: int32 [3072], P(('row', 'col')), may hold values from 0 to 8191, as said below
- q_blocks: bfloat16 [64, 48, 128, 128], P('col', 'row'), may hold values from -2 to 2
- q_cols: int32 [64, 48], P('col', 'row'), may hold values from 0 to 8191, as said below
Outputs:
- symmetric: float32 [64, 64, 128, 128], P('col', None, 'row')
The draws below stay inside these ranges and needn't reach their ends.
Inputs may be any that keep to these rules, and one draw needn't show every extreme that they name: For some c0 shared by x_cols and q_cols, the 48 block columns of window row i (in either array) are distinct and lie among the 128 columns (c0 + i + t) mod 8192, t = 0 ... 127. `q_cols`: as for x_cols, with the same c0.
All inputs are finite; a program needn't handle non-finite values.
Results may differ from the reference program's by a relative error of at most 0.00035.
Values may be sent and summed in bfloat16 or wider, within the bound.
A program may use at most 64 MiB of HBM per device.

```python
import jax
import jax.numpy as jnp
from jax import lax

BLK = 128
KB = 8192
NNZ = 48
NBH = 128
WB = 64


def pattern(key, salt):
    center = KB - WB // 2 - NBH // 2
    subkeys = jax.random.split(jax.random.fold_in(key, salt), WB)
    window_rows = jnp.arange(WB, dtype=jnp.int32)
    places = jnp.arange(NBH, dtype=jnp.int32)

    def one_row(subkey, row_number):
        scores = jax.random.randint(subkey, (NBH,), 0, 1048576)
        forced = (row_number == WB // 2) & ((places == NBH // 2 - 1) | (places == NBH // 2))
        scores = jnp.where(forced, -1, scores)
        return jnp.argsort(scores, stable=True)[:NNZ].astype(jnp.int32)
    offsets = jax.vmap(one_row)(subkeys, window_rows)
    return ((center + window_rows[:, None] + offsets) % KB).astype(jnp.int32)


def draw_x_cols(key, part):
    return pattern(key, 1).reshape(-1)


def draw_q_cols(key, part):
    own_pattern = pattern(key, 2)
    x_pattern = pattern(key, 1)
    key = jax.random.fold_in(key, 7)
    copied = jax.random.randint(jax.random.fold_in(key, 1), (WB,), 0, 4) == 0
    chosen_row = jax.random.randint(jax.random.fold_in(key, 2), (), 0, WB)
    copied = copied | (jnp.arange(WB, dtype=jnp.int32) == chosen_row)
    return jnp.where(copied[:, None], x_pattern, own_pattern).astype(jnp.int32)


def shard_levels(stream_key, shape, shards, low, high):
    level = 1.0
    for position, shards_of in shards:
        heights = jax.random.uniform(jax.random.fold_in(jax.random.fold_in(stream_key, 6), position), (shards_of,), jnp.float32, low / len(shards), high / len(shards))
        level = level * jnp.repeat(jnp.exp(heights), shape[position] // shards_of).reshape((-1,) + (1,) * (len(shape) - 1 - position))
    return level


def centred(key, shape, spread, most, shards=(), held_as=jnp.bfloat16):
    result = spread * jax.random.normal(key, shape, jnp.float32)
    if shards:
        result = result * shard_levels(key, shape, shards, -0.22, 0.18)
    return jnp.clip(result, -most, most).astype(held_as)


def setup_inputs(seed: int = 0) -> dict:
    splits = jax.random.split(jax.random.key(seed), 5)
    x_blocks = centred(splits[0], (WB * NNZ, BLK, BLK), 0.15, 2.0, ((0, 1024),))
    x_cols = draw_x_cols(jax.random.fold_in(splits[4], 71), 0)
    q_blocks = centred(splits[2], (WB, NNZ, BLK, BLK), 0.15, 2.0, ((0, 64), (1, 16)))
    q_cols = draw_q_cols(jax.random.fold_in(splits[4], 71), 0)
    return dict(x_blocks=x_blocks, x_cols=x_cols, q_blocks=q_blocks, q_cols=q_cols)


def reference(x_blocks, x_cols, q_blocks, q_cols):
    x_rows = x_blocks.reshape(WB, NNZ, BLK, BLK)
    x_index = x_cols.reshape(WB, NNZ)
    q_float = q_blocks.astype(jnp.float32)

    def one_row(inputs):
        blocks, columns = inputs
        match = (columns[:, None, None] == q_cols[None, :, :]).astype(jnp.float32)
        aligned = jnp.einsum('pjq,jqyz->jpyz', match, q_float, precision=lax.Precision.HIGHEST)
        return jnp.einsum('pxz,jpyz->jxy', blocks.astype(jnp.float32), aligned, precision=lax.Precision.HIGHEST)

    product = lax.map(one_row, (x_rows, x_index))
    return 0.5 * (product + jnp.transpose(product, (1, 0, 3, 2)))
```

```python
import functools

import jax
import jax.numpy as jnp
from jax import lax
from jax.experimental import pallas as pl
from jax.experimental.pallas import tpu as pltpu
from jax.sharding import PartitionSpec as P

MESH = pl.DeviceIdType.MESH
NZ = 32
STEPS = 16
V_AT = 5
WIN = 132
GROUP = 4


def where_am_i():
    row, col = lax.axis_index("row"), lax.axis_index("col")
    x, zh, core = row // 4, (row // 2) % 2, row % 2
    zl, y = col // 4, col % 4
    return x, y, zh, zl, core


def device(x, y, z, core):
    return (x * 4 + (z // 16) * 2 + core, (z % 16) * 4 + y)


def gather_kernel(xb, qb, meta, w, wm, v, vm, wp_send, wp_recv, v1_send, v1_recv,
                  v2_send, v2_recv, ring_send, ring_recv):
    x, y, zh, zl, core = where_am_i()
    z = zh * 16 + zl
    a = zl // 4
    me = device(x, y, z, core)
    chip = x * 4 + y

    def is_me(dev):
        return (dev[0] == me[0]) & (dev[1] == me[1])

    x_plane = 4 * x + 2 * zh + core
    x_dst = [device(zl % 4, y, x_plane + 16 * h, 1) for h in range(2)]
    q_dst = [device(x, y, zl + 16 * h, 0) for h in range(2)]

    bar = pltpu.get_barrier_semaphore()

    def greet(k, carry):
        chip2 = (chip + k // 2) % 16
        core2 = (core + k % 2) % 2
        pl.semaphore_signal(bar, inc=1, device_id=device(chip2 // 4, chip2 % 4, z, core2), device_id_type=MESH)
        return carry
    lax.fori_loop(1, 32, greet, 0)
    right = device(x, y, (z + 1) % NZ, core)
    left = device(x, y, (z + NZ - 1) % NZ, core)
    for dev in (right, left, device(x, y, (z + 16) % NZ, 0), device(x, y, (z + 16) % NZ, 1)):
        pl.semaphore_signal(bar, inc=1, device_id=dev, device_id_type=MESH)
    for b in range(4):
        src = (zl, (4 * b + x) * 4 + y)

        @pl.when((core == 1) & jnp.logical_not(is_me(src)))
        def _():
            pl.semaphore_signal(bar, inc=1, device_id=src, device_id_type=MESH)
    own_pieces = sum(jnp.where(is_me(dev), 1, 0) for dev in x_dst)
    pl.semaphore_wait(bar, 37 - own_pieces)

    sent = []

    def send(src, dst, ssem, rsem, dev):
        mine = is_me(dev)
        copy = pltpu.make_async_remote_copy(src, dst, ssem, rsem, device_id=dev, device_id_type=MESH)

        @pl.when(jnp.logical_not(mine))
        def _():
            copy.start()

        @pl.when(mine)
        def _():
            pltpu.make_async_copy(src, dst, rsem).start()
        sent.append((mine, copy))

    for s in range(4):
        x_to = device((x + a) % 4, s, z, 0)
        send(xb.at[:, s], w.at[z, y * 2 + core], wp_send.at[0, s, 0], wp_recv.at[0], x_to)
        send(meta.at[0], wm.at[z, y * 2 + core], wp_send.at[0, s, 1], wp_recv.at[1], x_to)
        q_to = device((y + a) % 4, s, z, 1)
        send(qb.at[:, s], w.at[z, x * 2 + core], wp_send.at[1, s, 0], wp_recv.at[0], q_to)
        send(meta.at[1], wm.at[z, x * 2 + core], wp_send.at[1, s, 1], wp_recv.at[1], q_to)
    for h in range(2):
        slot = (zl % 4) * 4 + y
        send(xb.at[:, :, h], v.at[slot, a], v1_send.at[0, h, 0], v1_recv.at[0], x_dst[h])
        send(meta.at[0], vm.at[slot, a], v1_send.at[0, h, 1], v1_recv.at[1], x_dst[h])
        part = zh * 2 + core
        send(qb.at[:, :, h], v.at[chip, part], v1_send.at[1, h, 0], v1_recv.at[0], q_dst[h])
        send(meta.at[1], vm.at[chip, part], v1_send.at[1, h, 1], v1_recv.at[1], q_dst[h])

    w[NZ] = jnp.zeros(w.shape[1:], w.dtype)
    v[16] = jnp.zeros(v.shape[1:], v.dtype)

    def ring(way, step, part):
        plane = (z + NZ - step) % NZ if way == 0 else (z + step) % NZ
        ref = wm.at[plane] if part == 2 else w.at[plane, pl.ds(part * 4, 4)]
        return pltpu.make_async_remote_copy(
            ref, ref, ring_send.at[way, step, part], ring_recv.at[way, step, part],
            device_id=right if way == 0 else left, device_id_type=MESH)

    def arrived(way, step, part):
        plane = (z + NZ - step - 1) % NZ if way == 0 else (z + step + 1) % NZ
        ref = wm.at[plane] if part == 2 else w.at[plane, pl.ds(part * 4, 4)]
        pltpu.make_async_copy(ref, ref, ring_recv.at[way, step, part]).wait()

    pltpu.make_async_copy(w.at[z], w.at[z], wp_recv.at[0]).wait()
    pltpu.make_async_copy(wm.at[z], wm.at[z], wp_recv.at[1]).wait()
    for part in range(3):
        for way in range(2):
            ring(way, 0, part).start()

    def ring_step(step, carry):
        for part in range(3):
            for way in range(2):
                arrived(way, step - 1, part)
                ring(way, step, part).start()
        return carry
    lax.fori_loop(1, V_AT, ring_step, 0)

    pltpu.make_async_copy(v.at[chip], v.at[chip], v1_recv.at[0]).wait()
    pltpu.make_async_copy(vm.at[chip], vm.at[chip], v1_recv.at[1]).wait()

    def share(k, n):
        chip2 = (chip + k) % 16
        ref = (v, vm)[n].at[chip]
        return pltpu.make_async_remote_copy(
            ref, ref, v2_send.at[k, n], v2_recv.at[chip, n],
            device_id=device(chip2 // 4, chip2 % 4, z, core), device_id_type=MESH)

    def share_start(k, carry):
        for n in range(2):
            share(k, n).start()
        return carry
    lax.fori_loop(1, 16, share_start, 0)

    lax.fori_loop(V_AT, STEPS - 1, ring_step, 0)
    last = STEPS - 1
    for way, part in ((0, 0), (1, 1), (0, 2)):
        arrived(way, last - 1, part)
        ring(way, last, part).start()
    for way, part in ((1, 0), (0, 1), (1, 2)):
        arrived(way, last - 1, part)

    def share_end(k, carry):
        chip2 = (chip + k) % 16
        for n in range(2):
            ref = (v, vm)[n].at[chip2]
            pltpu.make_async_copy(ref, ref, v2_recv.at[chip2, n]).wait()
            share(k, n).wait_send()
        return carry
    lax.fori_loop(1, 16, share_end, 0)
    for mine, copy in sent:
        @pl.when(jnp.logical_not(mine))
        def _():
            copy.wait_send()

    def ring_sent(step, carry):
        for part in range(3):
            for way in range(2):
                ring(way, step, part).wait_send()
        return carry
    lax.fori_loop(0, last, ring_sent, 0)
    for way, part in ((0, 0), (1, 1), (0, 2)):
        arrived(way, last, part)
        ring(way, last, part).wait_send()


def gather(xb, qb, meta):
    bf, i32 = jnp.bfloat16, jnp.int32
    dma = pltpu.SemaphoreType.DMA
    vmem = pl.BlockSpec(memory_space=pltpu.VMEM)
    return pl.pallas_call(
        gather_kernel,
        out_shape=(
            jax.ShapeDtypeStruct((NZ + 1, 8, 3, 2, 16, 128), bf),
            jax.ShapeDtypeStruct((NZ, 8, 1, 128), i32),
            jax.ShapeDtypeStruct((17, 4, 3, 4, 16, 128), bf),
            jax.ShapeDtypeStruct((16, 4, 1, 128), i32),
        ),
        in_specs=[vmem] * 3,
        out_specs=(vmem,) * 4,
        scratch_shapes=[
            dma((2, 4, 2)), dma((2,)), dma((2, 2, 2)), dma((2,)),
            dma((16, 2)), dma((16, 2)), dma((2, STEPS, 3)), dma((2, STEPS, 3)),
        ],
        compiler_params=pltpu.CompilerParams(
            collective_id=0, has_side_effects=True, vmem_limit_bytes=40 * 2**20),
        name="gather",
    )(xb, qb, meta)


def tables(wm, vm):
    core = lax.axis_index("row") % 2
    w_cols = wm[:, :, 0, :3]
    v_cols = vm[:, :, 0, :3]
    w_ids = jnp.arange(NZ * 24, dtype=jnp.int32)
    v_ids = jnp.arange(192, dtype=jnp.int32)

    def rows_w(t):
        from_x = t.reshape(2, 4, 4, 4, 2, 3).transpose(1, 0, 4, 2, 3, 5).reshape(16, 48)
        from_q = t.reshape(2, 4, 4, 24).transpose(1, 2, 0, 3).reshape(16, 48)
        return jnp.where(core == 0, from_x, from_q)

    def rows_v(t):
        from_q = t.reshape(4, 4, 12).transpose(1, 0, 2).reshape(4, 48)
        from_x = t.reshape(16, 4, 3).transpose(1, 0, 2).reshape(4, 48)
        return jnp.where(core == 0, from_q, from_x)
    wc, wi = rows_w(w_cols), rows_w(w_ids)
    vc, vi = rows_v(v_cols), rows_v(v_ids)
    first = vc[0, 0]
    off = ((vc - first + 4096) & 8191) - 4096 - jnp.arange(4, dtype=jnp.int32)[:, None]
    base = first + jnp.min(off)
    places = jnp.arange(WIN, dtype=jnp.int32)

    def table(cols, ids, none):
        hit = ((cols - base) & 8191)[:, :, None] == places
        return none + jnp.sum(jnp.where(hit, ids[:, :, None] - none, 0), axis=1)
    return table(vc, vi, 192), table(wc, wi, NZ * 24)


def product_kernel(tv, tw, v, w, out):
    out[...] = jnp.zeros_like(out)

    def step(g, carry):
        vs, ws = [], []
        for u in range(GROUP):
            at = g * GROUP + u
            vs.append(jnp.concatenate([v[tv[c, at]].reshape(64, 128) for c in range(4)], axis=0))
            ws.append(jnp.concatenate([w[tw[m, at]].reshape(32, 128) for m in range(16)], axis=0))
        left = jnp.concatenate(vs, axis=1)
        right = jnp.concatenate(ws, axis=1)
        out[...] += lax.dot_general(left, right, (((1,), (1,)), ((), ())), preferred_element_type=jnp.float32)
        return carry
    lax.fori_loop(0, WIN // GROUP, step, 0)


def product(tv, tw, v, w):
    vmem = pl.BlockSpec(memory_space=pltpu.VMEM)
    smem = pl.BlockSpec(memory_space=pltpu.SMEM)
    return pl.pallas_call(
        product_kernel,
        out_shape=jax.ShapeDtypeStruct((256, 512), jnp.float32),
        in_specs=[smem, smem, vmem, vmem],
        out_specs=vmem,
        compiler_params=pltpu.CompilerParams(vmem_limit_bytes=40 * 2**20),
        name="product",
    )(tv, tw, v, w)


def exchange_kernel(t, out, got, send_sem, recv_sem):
    x, y, zh, zl, core = where_am_i()
    z = zh * 16 + zl
    chip = x * 4 + y
    mine = chip * 2 + core
    bar = pltpu.get_barrier_semaphore()

    def peer(k):
        other = (mine + k) % 32
        px, py, pc = other // 8, (other // 2) % 4, other % 2
        return other, px, py, pc

    def greet(k, carry):
        _, px, py, pc = peer(k)
        pl.semaphore_signal(bar, inc=1, device_id=device(px, py, z, pc), device_id_type=MESH)
        return carry
    lax.fori_loop(1, 32, greet, 0)
    pl.semaphore_wait(bar, 31)

    def copy(k):
        _, px, py, pc = peer(k)
        return pltpu.make_async_remote_copy(
            t.at[py, px, pc], got.at[mine], send_sem.at[k], recv_sem.at[mine],
            device_id=device(px, py, z, pc), device_id_type=MESH)

    def start(k, carry):
        copy(k).start()
        return carry
    lax.fori_loop(1, 32, start, 0)
    own = pltpu.make_async_copy(t.at[y, x, core], got.at[mine], recv_sem.at[mine])
    own.start()
    own.wait()

    def finish(k, carry):
        other, _, _, _ = peer(k)
        pltpu.make_async_copy(got.at[other], got.at[other], recv_sem.at[other]).wait()
        copy(k).wait_send()
        return carry
    lax.fori_loop(1, 32, finish, 0)

    lane = lax.broadcasted_iota(jnp.int32, (8, 128), 1) // 32
    for xs in range(4):
        halves = []
        for cs in range(2):
            rows = {}
            for m4 in range(4):
                part = [got[(xs * 4 + ys) * 2 + cs, :, m4 * 128:(m4 + 1) * 128] for ys in range(4)]
                for mid in range(4):
                    acc = None
                    for ys in range(4):
                        turn = ((ys - mid) * 32) % 128
                        piece = pltpu.roll(part[ys], turn, axis=1) if turn else part[ys]
                        acc = piece if acc is None else jnp.where(lane == ys, piece, acc)
                    if cs == 0:
                        j = 16 * ((xs - m4) % 4) + 4 * mid + m4
                    else:
                        j = 16 * m4 + 4 * mid + (xs - m4) % 4
                    rows[j] = acc
            halves.append(rows)
        for j in halves[0]:
            out[j] = 0.5 * (halves[0][j] + halves[1][j])


def exchange(t):
    dma = pltpu.SemaphoreType.DMA
    vmem = pl.BlockSpec(memory_space=pltpu.VMEM)
    return pl.pallas_call(
        exchange_kernel,
        out_shape=jax.ShapeDtypeStruct((64, 8, 128), jnp.float32),
        in_specs=[vmem],
        out_specs=vmem,
        scratch_shapes=[pltpu.VMEM((32, 8, 512), jnp.float32), dma((32,)), dma((32,))],
        compiler_params=pltpu.CompilerParams(
            collective_id=1, has_side_effects=True, vmem_limit_bytes=16 * 2**20),
        name="exchange",
    )(t)


def shards(x_blocks, x_cols, q_blocks, q_cols):
    xb = x_blocks.reshape(3, 4, 2, 16, 128)
    qb = q_blocks.reshape(3, 4, 2, 16, 128)
    meta = jnp.pad(jnp.stack([x_cols, q_cols[0]]), ((0, 0), (0, 125))).reshape(2, 1, 128)
    w, wm, v, vm = gather(xb, qb, meta)
    tv, tw = tables(wm, vm)
    t = product(tv, tw, v.reshape(17 * 12, 4, 16, 128), w.reshape((NZ + 1) * 24, 2, 16, 128))
    return exchange(t.reshape(4, 4, 2, 8, 512))[None]


def solution(mesh):
    placed = (
        P(("row", "col"), None, None),
        P(("row", "col")),
        P("col", "row", None, None),
        P("col", "row"),
    )
    return jax.shard_map(
        shards, mesh=mesh, in_specs=placed, out_specs=P("col", None, "row", None), check_vma=False
    )
```

```python
import jax
import jax.numpy as jnp
from jax import lax
from jax.experimental import pallas as pl
from jax.experimental.pallas import tpu as pltpu
from jax.sharding import PartitionSpec as P

MESH = pl.DeviceIdType.MESH
NZ = 32
STEPS = 16
PARTS = 4
WIN = 132
GROUP = 4


def where_am_i():
    row, col = lax.axis_index("row"), lax.axis_index("col")
    x, zh, core = row // 4, (row // 2) % 2, row % 2
    zl, y = col // 4, col % 4
    return x, y, zh, zl, core


def device(x, y, z, core):
    return (x * 4 + (z // 16) * 2 + core, (z % 16) * 4 + y)


def gather_kernel(xb, qb, meta, w, wm, v, vm, w_send, w_recv, v_send, v_recv, ring_send, ring_recv):
    x, y, zh, zl, core = where_am_i()
    z = zh * 16 + zl
    a = zl // 4
    me = device(x, y, z, core)
    chip = x * 4 + y
    right = device(x, y, (z + 1) % NZ, core)
    left = device(x, y, (z + NZ - 1) % NZ, core)

    def is_me(dev):
        return (dev[0] == me[0]) & (dev[1] == me[1])

    bar = pltpu.get_barrier_semaphore()

    def greet(k, carry):
        chip2 = (chip + k // 2) % 16
        core2 = (core + k % 2) % 2
        pl.semaphore_signal(bar, inc=1, device_id=device(chip2 // 4, chip2 % 4, z, core2), device_id_type=MESH)
        return carry
    lax.fori_loop(1, 32, greet, 0)
    for dev in (right, left):
        pl.semaphore_signal(bar, inc=1, device_id=dev, device_id_type=MESH)
    pl.semaphore_wait(bar, 33)

    sent = []

    def send(src, dst, ssem, rsem, dev):
        mine = is_me(dev)
        copy = pltpu.make_async_remote_copy(src, dst, ssem, rsem, device_id=dev, device_id_type=MESH)

        @pl.when(jnp.logical_not(mine))
        def _():
            copy.start()

        @pl.when(mine)
        def _():
            pltpu.make_async_copy(src, dst, rsem).start()
        sent.append((mine, copy))

    for s in range(4):
        x_to = device((x + a) % 4, s, z, 0)
        send(xb.at[:, s], w.at[z, y * 2 + core], w_send.at[0, s, 0], w_recv.at[0], x_to)
        send(meta.at[0], wm.at[z, y * 2 + core], w_send.at[0, s, 1], w_recv.at[1], x_to)
        q_to = device((y + a) % 4, s, z, 1)
        send(qb.at[:, s], w.at[z, x * 2 + core], w_send.at[1, s, 0], w_recv.at[0], q_to)
        send(meta.at[1], wm.at[z, x * 2 + core], w_send.at[1, s, 1], w_recv.at[1], q_to)

    w[NZ] = jnp.zeros(w.shape[1:], w.dtype)
    v[64] = jnp.zeros(v.shape[1:], v.dtype)

    size = 8 // PARTS

    def chunk(plane, part):
        return wm.at[plane] if part == PARTS else w.at[plane, pl.ds(part * size, size)]

    def ring(way, step, part):
        ref = chunk((z + NZ - step) % NZ if way == 0 else (z + step) % NZ, part)
        return pltpu.make_async_remote_copy(
            ref, ref, ring_send.at[way, step, part], ring_recv.at[way, step, part],
            device_id=right if way == 0 else left, device_id_type=MESH)

    def arrived(way, step, part):
        ref = chunk((z + NZ - step - 1) % NZ if way == 0 else (z + step + 1) % NZ, part)
        pltpu.make_async_copy(ref, ref, ring_recv.at[way, step, part]).wait()

    own = (x + 4 - a) % 4

    def pass_on(plane):
        half, quarter, place = plane // 16, (plane % 16) // 4, plane % 4

        @pl.when((core == 0) & (half == (zl // 2) % 2) & (quarter == own))
        def _():
            def one(k, carry):
                chip2 = (chip + k) % 16
                to = device(chip2 // 4, chip2 % 4, z, 1)
                for yy in range(4):
                    g = quarter * 16 + place * 4 + yy
                    pltpu.make_async_remote_copy(
                        w.at[plane, yy * 2 + zl % 2, :, zh], v.at[g, :, y], v_send.at[0], v_recv.at[0],
                        device_id=to, device_id_type=MESH).start()

                    @pl.when(chip2 % 4 == y)
                    def _():
                        pltpu.make_async_remote_copy(
                            wm.at[plane, yy * 2 + zl % 2], vm.at[g], v_send.at[1], v_recv.at[1],
                            device_id=to, device_id_type=MESH).start()
                return carry
            lax.fori_loop(0, 16, one, 0)

        @pl.when((core == 1) & (plane % 16 == zl))
        def _():
            def one(k, carry):
                chip2 = (chip + k) % 16
                to = device(chip2 // 4, chip2 % 4, z, 0)
                g = own * 16 + half * 8
                pltpu.make_async_remote_copy(
                    w.at[plane, :, :, zh], v.at[pl.ds(g, 8), :, y], v_send.at[0], v_recv.at[0],
                    device_id=to, device_id_type=MESH).start()

                @pl.when(chip2 % 4 == y)
                def _():
                    pltpu.make_async_remote_copy(
                        wm.at[plane], vm.at[pl.ds(g, 8)], v_send.at[1], v_recv.at[1],
                        device_id=to, device_id_type=MESH).start()
                return carry
            lax.fori_loop(0, 16, one, 0)

    pltpu.make_async_copy(w.at[z], w.at[z], w_recv.at[0]).wait()
    pltpu.make_async_copy(wm.at[z], wm.at[z], w_recv.at[1]).wait()
    for part in range(PARTS + 1):
        for way in range(2):
            ring(way, 0, part).start()
    pass_on(z)

    def ring_step(step, carry):
        for part in range(PARTS + 1):
            for way in range(2):
                arrived(way, step - 1, part)
                ring(way, step, part).start()
        pass_on((z + NZ - step) % NZ)
        pass_on((z + step) % NZ)
        return carry
    last = STEPS - 1
    lax.fori_loop(1, last, ring_step, 0)
    ends = [(0 if part < PARTS // 2 else 1, part) for part in range(PARTS + 1)]
    for way, part in ends:
        arrived(way, last - 1, part)
        ring(way, last, part).start()
    for way, part in ends:
        arrived(1 - way, last - 1, part)
    pass_on((z + NZ - last) % NZ)
    pass_on((z + last) % NZ)
    for way, part in ends:
        arrived(way, last, part)
    pass_on((z + 16) % NZ)

    for mine, copy in sent:
        @pl.when(jnp.logical_not(mine))
        def _():
            copy.wait_send()

    def ring_sent(step, carry):
        for part in range(PARTS + 1):
            for way in range(2):
                ring(way, step, part).wait_send()
        return carry
    lax.fori_loop(0, last, ring_sent, 0)
    for way, part in ends:
        ring(way, last, part).wait_send()
    rows = v.at[pl.ds(0, 64)]
    for n, ref in enumerate((rows, vm)):
        pltpu.make_async_copy(ref, ref, v_recv.at[n]).wait()
        pltpu.make_async_copy(ref, ref, v_send.at[n]).wait()


def gather(xb, qb, meta):
    bf, i32 = jnp.bfloat16, jnp.int32
    dma = pltpu.SemaphoreType.DMA
    vmem = pl.BlockSpec(memory_space=pltpu.VMEM)
    return pl.pallas_call(
        gather_kernel,
        out_shape=(
            jax.ShapeDtypeStruct((NZ + 1, 8, 3, 2, 16, 128), bf),
            jax.ShapeDtypeStruct((NZ, 8, 1, 128), i32),
            jax.ShapeDtypeStruct((65, 3, 4, 16, 128), bf),
            jax.ShapeDtypeStruct((64, 1, 128), i32),
        ),
        in_specs=[vmem] * 3,
        out_specs=(vmem,) * 4,
        scratch_shapes=[
            dma((2, 4, 2)), dma((2,)), dma((2,)), dma((2,)),
            dma((2, STEPS, PARTS + 1)), dma((2, STEPS, PARTS + 1)),
        ],
        compiler_params=pltpu.CompilerParams(
            collective_id=0, has_side_effects=True, vmem_limit_bytes=40 * 2**20),
        name="gather",
    )(xb, qb, meta)


def product_kernel(wm, vm, v_hbm, w_hbm, out, v, w, rows, tab, v_sem, w_sem, tab_sem):
    x, y, zh, zl, core = where_am_i()
    v_in = pltpu.make_async_copy(v_hbm, v, v_sem)
    w_in = pltpu.make_async_copy(w_hbm, w, w_sem)
    v_in.start()
    w_in.start()

    v_cols, w_cols = vm[...], wm[...]
    first = v_cols[0:1, 0:1]
    row = lax.broadcasted_iota(jnp.int32, (64, 128), 0) // 16
    lane = lax.broadcasted_iota(jnp.int32, (64, 128), 1)
    off = ((v_cols - first + 4096) & 8191) - 4096 - row
    off = jnp.where(lane < 3, off, 8192).astype(jnp.float32)
    least = jnp.min(jnp.min(off, axis=1, keepdims=True), axis=0, keepdims=True)
    base = first + least.astype(jnp.int32)

    def hits(cols, none):
        n = cols.shape[0]
        place = lax.broadcasted_iota(jnp.int32, (n, 256), 1)
        ids = (lax.broadcasted_iota(jnp.int32, (n, 256), 0) * 3 - none).astype(jnp.float32)
        total = jnp.zeros((n, 256), jnp.float32)
        for k in range(3):
            total += jnp.where(((cols[:, k:k + 1] - base) & 8191) == place, ids + k, 0.0)
        return total

    none_v, none_w = 192, NZ * 24
    in_v = jnp.sum(hits(v_cols, none_v).reshape(4, 16, 256), axis=1)
    in_w = hits(w_cols, none_w).reshape(2, 4, 4, 8, 256)
    from_q = jnp.sum(jnp.sum(in_w, axis=0), axis=2)
    over_place = in_w[:, :, 0] + in_w[:, :, 1] + in_w[:, :, 2] + in_w[:, :, 3]
    odd = lax.broadcasted_iota(jnp.int32, (2, 4, 8, 256), 2) % 2
    from_x = [jnp.sum(jnp.where(odd == n, over_place, 0.0), axis=2) for n in range(2)]
    for b in range(4):
        for mid in range(4):
            of_x = from_x[mid % 2][mid // 2, b:b + 1]
            of_q = from_q[(3 - b) % 4, mid:mid + 1]
            for xs in range(3):
                of_q = jnp.where(x == xs, from_q[(xs - b) % 4, mid:mid + 1], of_q)
            m = b * 4 + mid
            rows[m:m + 1] = jnp.where(core == 0, of_x, of_q).astype(jnp.int32) + none_w
    rows[16:20] = in_v.astype(jnp.int32) + none_v
    tab_in = pltpu.make_async_copy(rows, tab, tab_sem)
    tab_in.start()
    out[...] = jnp.zeros_like(out)
    tab_in.wait()
    v_in.wait()
    w_in.wait()

    def step(g, carry):
        vs, ws = [], []
        for u in range(GROUP):
            at = g * GROUP + u
            vs.append(jnp.concatenate([v[tab[16 + c, at]].reshape(64, 128) for c in range(4)], axis=0))
            ws.append(jnp.concatenate([w[tab[m, at]].reshape(32, 128) for m in range(16)], axis=0))
        left = jnp.concatenate(vs, axis=1)
        right = jnp.concatenate(ws, axis=1)
        out[...] += lax.dot_general(left, right, (((1,), (1,)), ((), ())), preferred_element_type=jnp.float32)
        return carry
    lax.fori_loop(0, WIN // GROUP, step, 0)


def product(wm, vm, v, w):
    vmem = pl.BlockSpec(memory_space=pltpu.VMEM)
    hbm = pl.BlockSpec(memory_space=pl.ANY)
    dma = pltpu.SemaphoreType.DMA
    return pl.pallas_call(
        product_kernel,
        out_shape=jax.ShapeDtypeStruct((256, 512), jnp.float32),
        in_specs=[vmem, vmem, hbm, hbm],
        out_specs=vmem,
        scratch_shapes=[
            pltpu.VMEM(v.shape, v.dtype), pltpu.VMEM(w.shape, w.dtype),
            pltpu.VMEM((24, 256), jnp.int32), pltpu.SMEM((24, 256), jnp.int32),
            dma, dma, dma,
        ],
        compiler_params=pltpu.CompilerParams(vmem_limit_bytes=40 * 2**20),
        name="product",
    )(wm, vm, v, w)


def exchange_kernel(t, out, half, total, got, half_send, half_recv, send_sem, recv_sem):
    x, y, zh, zl, core = where_am_i()
    z = zh * 16 + zl
    chip = x * 4 + y
    bar = pltpu.get_barrier_semaphore()

    def greet(k, carry):
        chip2 = (chip + k) % 16
        pl.semaphore_signal(bar, inc=1, device_id=device(chip2 // 4, chip2 % 4, z, core), device_id_type=MESH)
        return carry
    lax.fori_loop(1, 16, greet, 0)
    partner = device(x, y, z, 1 - core)
    pl.semaphore_signal(bar, inc=1, device_id=partner, device_id_type=MESH)
    pl.semaphore_wait(bar, 16)

    swap = pltpu.make_async_remote_copy(
        t.at[:, :, 1 - core], half, half_send, half_recv, device_id=partner, device_id_type=MESH)
    swap.start()
    swap.wait_recv()
    total[...] = t[:, :, core] + half[...]

    def copy(k):
        chip2 = (chip + k) % 16
        return pltpu.make_async_remote_copy(
            total.at[chip2 % 4, chip2 // 4], got.at[chip], send_sem.at[k], recv_sem.at[chip],
            device_id=device(chip2 // 4, chip2 % 4, z, core), device_id_type=MESH)

    def start(k, carry):
        copy(k).start()
        return carry
    lax.fori_loop(1, 16, start, 0)
    own = pltpu.make_async_copy(total.at[y, x], got.at[chip], recv_sem.at[chip])
    own.start()
    own.wait()
    swap.wait_send()

    def finish(k, carry):
        chip2 = (chip + k) % 16
        pltpu.make_async_copy(got.at[chip2], got.at[chip2], recv_sem.at[chip2]).wait()
        copy(k).wait_send()
        return carry
    lax.fori_loop(1, 16, finish, 0)

    lane = lax.broadcasted_iota(jnp.int32, (8, 128), 1) // 32
    for xs in range(4):
        for b in range(4):
            part = [got[xs * 4 + ys, :, b * 128:(b + 1) * 128] for ys in range(4)]
            for mid in range(4):
                acc = None
                for ys in range(4):
                    turn = ((ys - mid) * 32) % 128
                    piece = pltpu.roll(part[ys], turn, axis=1) if turn else part[ys]
                    acc = piece if acc is None else jnp.where(lane == ys, piece, acc)
                out[16 * ((xs - b) % 4) + 4 * mid + b] = 0.5 * acc


def exchange(t):
    dma = pltpu.SemaphoreType.DMA
    vmem = pl.BlockSpec(memory_space=pltpu.VMEM)
    f32 = jnp.float32
    return pl.pallas_call(
        exchange_kernel,
        out_shape=jax.ShapeDtypeStruct((64, 8, 128), f32),
        in_specs=[vmem],
        out_specs=vmem,
        scratch_shapes=[
            pltpu.VMEM((4, 4, 8, 512), f32), pltpu.VMEM((4, 4, 8, 512), f32), pltpu.VMEM((16, 8, 512), f32),
            dma, dma, dma((16,)), dma((16,)),
        ],
        compiler_params=pltpu.CompilerParams(
            collective_id=1, has_side_effects=True, vmem_limit_bytes=16 * 2**20),
        name="exchange",
    )(t)


def shards(x_blocks, x_cols, q_blocks, q_cols):
    xb = x_blocks.reshape(3, 4, 2, 16, 128)
    qb = q_blocks.reshape(3, 4, 2, 16, 128)
    meta = jnp.pad(jnp.stack([x_cols, q_cols[0]]), ((0, 0), (0, 125))).reshape(2, 1, 128)
    w, wm, v, vm = gather(xb, qb, meta)
    t = product(
        wm.reshape(NZ * 8, 128), vm.reshape(64, 128),
        v.reshape(65 * 3, 4, 16, 128), w.reshape((NZ + 1) * 24, 2, 16, 128))
    return exchange(t.reshape(4, 4, 2, 8, 512))[None]


def solution(mesh):
    placed = (
        P(("row", "col"), None, None),
        P(("row", "col")),
        P("col", "row", None, None),
        P("col", "row"),
    )
    return jax.shard_map(
        shards, mesh=mesh, in_specs=placed, out_specs=P("col", None, "row", None), check_vma=False
    )
```

```python
import jax
import jax.numpy as jnp
from jax import lax
from jax.experimental import pallas as pl
from jax.experimental.pallas import tpu as pltpu
from jax.sharding import PartitionSpec as P

MESH = pl.DeviceIdType.MESH
NZ = 32
STEPS = 16
PARTS = 4
WIN = 132
GROUP = 33


def where_am_i():
    row, col = lax.axis_index("row"), lax.axis_index("col")
    x, zh, core = row // 4, (row // 2) % 2, row % 2
    zl, y = col // 4, col % 4
    return x, y, zh, zl, core


def device(x, y, z, core):
    return (x * 4 + (z // 16) * 2 + core, (z % 16) * 4 + y)


def gather_kernel(xb, qb, meta, w, wm, v, vm, w_send, w_recv, v_send, v_recv, ring_send, ring_recv):
    x, y, zh, zl, core = where_am_i()
    z = zh * 16 + zl
    a = zl // 4
    me = device(x, y, z, core)
    chip = x * 4 + y
    right = device(x, y, (z + 1) % NZ, core)
    left = device(x, y, (z + NZ - 1) % NZ, core)

    def is_me(dev):
        return (dev[0] == me[0]) & (dev[1] == me[1])

    bar = pltpu.get_barrier_semaphore()

    def greet(k, carry):
        chip2 = (chip + k // 2) % 16
        core2 = (core + k % 2) % 2
        pl.semaphore_signal(bar, inc=1, device_id=device(chip2 // 4, chip2 % 4, z, core2), device_id_type=MESH)
        return carry
    lax.fori_loop(1, 32, greet, 0)
    for dev in (right, left):
        pl.semaphore_signal(bar, inc=1, device_id=dev, device_id_type=MESH)
    pl.semaphore_wait(bar, 33)

    sent = []

    def send(src, dst, ssem, rsem, dev):
        mine = is_me(dev)
        copy = pltpu.make_async_remote_copy(src, dst, ssem, rsem, device_id=dev, device_id_type=MESH)

        @pl.when(jnp.logical_not(mine))
        def _():
            copy.start()

        @pl.when(mine)
        def _():
            pltpu.make_async_copy(src, dst, rsem).start()
        sent.append((mine, copy))

    for s in range(4):
        x_to = device((x + a) % 4, s, z, 0)
        send(xb.at[:, s], w.at[z, core * 4 + y], w_send.at[0, s, 0], w_recv.at[0], x_to)
        send(meta.at[0], wm.at[z, core * 4 + y], w_send.at[0, s, 1], w_recv.at[1], x_to)
        q_to = device((y + a) % 4, s, z, 1)
        send(qb.at[:, s], w.at[z, x * 2 + core], w_send.at[1, s, 0], w_recv.at[0], q_to)
        send(meta.at[1], wm.at[z, x * 2 + core], w_send.at[1, s, 1], w_recv.at[1], q_to)

    w[NZ] = jnp.zeros(w.shape[1:], w.dtype)
    v[64] = jnp.zeros(v.shape[1:], v.dtype)

    size = 8 // PARTS

    def chunk(plane, part):
        return wm.at[plane] if part == PARTS else w.at[plane, pl.ds(part * size, size)]

    def ring(way, step, part):
        ref = chunk((z + NZ - step) % NZ if way == 0 else (z + step) % NZ, part)
        return pltpu.make_async_remote_copy(
            ref, ref, ring_send.at[way, step, part], ring_recv.at[way, step, part],
            device_id=right if way == 0 else left, device_id_type=MESH)

    def arrived(way, step, part):
        ref = chunk((z + NZ - step - 1) % NZ if way == 0 else (z + step + 1) % NZ, part)
        pltpu.make_async_copy(ref, ref, ring_recv.at[way, step, part]).wait()

    own = (x + 4 - a) % 4

    def pass_on(plane):
        half, quarter, place = plane // 16, (plane % 16) // 4, plane % 4

        @pl.when((core == 0) & (half == (zl // 2) % 2) & (quarter == own))
        def _():
            def one(k, carry):
                chip2 = (chip + k) % 16
                to = device(chip2 // 4, chip2 % 4, z, 1)
                g = quarter * 16 + place * 4
                mine = pl.ds(zl % 2 * 4, 4)
                pltpu.make_async_remote_copy(
                    w.at[plane, mine, :, zh], v.at[pl.ds(g, 4), :, y], v_send.at[0], v_recv.at[0],
                    device_id=to, device_id_type=MESH).start()

                @pl.when(chip2 % 4 == y)
                def _():
                    pltpu.make_async_remote_copy(
                        wm.at[plane, mine], vm.at[pl.ds(g, 4)], v_send.at[1], v_recv.at[1],
                        device_id=to, device_id_type=MESH).start()
                return carry
            lax.fori_loop(0, 16, one, 0)

        @pl.when((core == 1) & (plane % 16 == zl))
        def _():
            def one(k, carry):
                chip2 = (chip + k) % 16
                to = device(chip2 // 4, chip2 % 4, z, 0)
                g = own * 16 + half * 8
                pltpu.make_async_remote_copy(
                    w.at[plane, :, :, zh], v.at[pl.ds(g, 8), :, y], v_send.at[0], v_recv.at[0],
                    device_id=to, device_id_type=MESH).start()

                @pl.when(chip2 % 4 == y)
                def _():
                    pltpu.make_async_remote_copy(
                        wm.at[plane], vm.at[pl.ds(g, 8)], v_send.at[1], v_recv.at[1],
                        device_id=to, device_id_type=MESH).start()
                return carry
            lax.fori_loop(0, 16, one, 0)

    pltpu.make_async_copy(w.at[z], w.at[z], w_recv.at[0]).wait()
    pltpu.make_async_copy(wm.at[z], wm.at[z], w_recv.at[1]).wait()
    for part in range(PARTS + 1):
        for way in range(2):
            ring(way, 0, part).start()
    pass_on(z)

    def ring_step(step, carry):
        for part in range(PARTS + 1):
            for way in range(2):
                arrived(way, step - 1, part)
                ring(way, step, part).start()
        pass_on((z + NZ - step) % NZ)
        pass_on((z + step) % NZ)
        return carry
    last = STEPS - 1
    lax.fori_loop(1, last, ring_step, 0)
    ends = [(0 if part < PARTS // 2 else 1, part) for part in range(PARTS + 1)]
    for way, part in ends:
        arrived(way, last - 1, part)
        ring(way, last, part).start()
    for way, part in ends:
        arrived(1 - way, last - 1, part)
    pass_on((z + NZ - last) % NZ)
    pass_on((z + last) % NZ)
    for way, part in ends:
        arrived(way, last, part)
    pass_on((z + 16) % NZ)

    for mine, copy in sent:
        @pl.when(jnp.logical_not(mine))
        def _():
            copy.wait_send()

    def ring_sent(step, carry):
        for part in range(PARTS + 1):
            for way in range(2):
                ring(way, step, part).wait_send()
        return carry
    lax.fori_loop(0, last, ring_sent, 0)
    for way, part in ends:
        ring(way, last, part).wait_send()
    rows = v.at[pl.ds(0, 64)]
    for n, ref in enumerate((rows, vm)):
        pltpu.make_async_copy(ref, ref, v_recv.at[n]).wait()
        pltpu.make_async_copy(ref, ref, v_send.at[n]).wait()


def gather(xb, qb, meta):
    bf, i32 = jnp.bfloat16, jnp.int32
    dma = pltpu.SemaphoreType.DMA
    vmem = pl.BlockSpec(memory_space=pltpu.VMEM)
    hbm = pl.BlockSpec(memory_space=pltpu.HBM)
    return pl.pallas_call(
        gather_kernel,
        out_shape=(
            jax.ShapeDtypeStruct((NZ + 1, 8, 3, 2, 16, 128), bf),
            jax.ShapeDtypeStruct((NZ, 8, 1, 128), i32),
            jax.ShapeDtypeStruct((65, 3, 4, 16, 128), bf),
            jax.ShapeDtypeStruct((64, 1, 128), i32),
        ),
        in_specs=[hbm, hbm, vmem],
        out_specs=(vmem,) * 4,
        scratch_shapes=[
            dma((2, 4, 2)), dma((2,)), dma((2,)), dma((2,)),
            dma((2, STEPS, PARTS + 1)), dma((2, STEPS, PARTS + 1)),
        ],
        compiler_params=pltpu.CompilerParams(
            collective_id=0, has_side_effects=True, vmem_limit_bytes=40 * 2**20),
        name="gather",
    )(xb, qb, meta)


def product_kernel(wm, vm, v, w, out, rows, tab, tab_sem):
    x, y, zh, zl, core = where_am_i()

    v_cols, w_cols = vm[...], wm[...]
    first = v_cols[0:1, 0:1]
    row = lax.broadcasted_iota(jnp.int32, (64, 128), 0) // 16
    lane = lax.broadcasted_iota(jnp.int32, (64, 128), 1)
    off = ((v_cols - first + 4096) & 8191) - 4096 - row
    off = jnp.where(lane < 3, off, 8192).astype(jnp.float32)
    least = jnp.min(jnp.min(off, axis=1, keepdims=True), axis=0, keepdims=True)
    base = first + least.astype(jnp.int32)

    def hits(cols, none):
        n = cols.shape[0]
        place = lax.broadcasted_iota(jnp.int32, (n, 256), 1)
        ids = (lax.broadcasted_iota(jnp.int32, (n, 256), 0) * 3 - none).astype(jnp.float32)
        total = jnp.zeros((n, 256), jnp.float32)
        for k in range(3):
            total += jnp.where(((cols[:, k:k + 1] - base) & 8191) == place, ids + k, 0.0)
        return total

    none_v, none_w = 192, NZ * 24
    in_v = jnp.sum(hits(v_cols, none_v).reshape(4, 16, 256), axis=1)
    in_w = hits(w_cols, none_w).reshape(2, 4, 4, 8, 256)
    from_q = jnp.sum(jnp.sum(in_w, axis=0), axis=2)
    over_place = in_w[:, :, 0] + in_w[:, :, 1] + in_w[:, :, 2] + in_w[:, :, 3]
    of_core = lax.broadcasted_iota(jnp.int32, (2, 4, 8, 256), 2) // 4
    from_x = [jnp.sum(jnp.where(of_core == n, over_place, 0.0), axis=2) for n in range(2)]
    for b in range(4):
        for mid in range(4):
            of_x = from_x[mid % 2][mid // 2, b:b + 1]
            of_q = from_q[(3 - b) % 4, mid:mid + 1]
            for xs in range(3):
                of_q = jnp.where(x == xs, from_q[(xs - b) % 4, mid:mid + 1], of_q)
            m = b * 4 + mid
            rows[m:m + 1] = jnp.where(core == 0, of_x, of_q).astype(jnp.int32) + none_w
    rows[16:20] = in_v.astype(jnp.int32) + none_v
    tab_in = pltpu.make_async_copy(rows, tab, tab_sem)
    tab_in.start()
    out[...] = jnp.zeros_like(out)
    tab_in.wait()

    def step(g, carry):
        vs, ws = [], []
        for u in range(GROUP):
            at = g * GROUP + u
            vs.append(jnp.concatenate([v[tab[16 + c, at]].reshape(64, 128) for c in range(4)], axis=0))
            ws.append(jnp.concatenate([w[tab[m, at]].reshape(32, 128) for m in range(16)], axis=0))
        left = jnp.concatenate(vs, axis=1)
        right = jnp.concatenate(ws, axis=1)
        out[...] += lax.dot_general(left, right, (((1,), (1,)), ((), ())), preferred_element_type=jnp.float32)
        return carry
    lax.fori_loop(0, WIN // GROUP, step, 0)


def product(wm, vm, v, w):
    vmem = pl.BlockSpec(memory_space=pltpu.VMEM)
    return pl.pallas_call(
        product_kernel,
        out_shape=jax.ShapeDtypeStruct((256, 512), jnp.float32),
        in_specs=[vmem] * 4,
        out_specs=vmem,
        scratch_shapes=[
            pltpu.VMEM((24, 256), jnp.int32), pltpu.SMEM((24, 256), jnp.int32),
            pltpu.SemaphoreType.DMA,
        ],
        compiler_params=pltpu.CompilerParams(vmem_limit_bytes=40 * 2**20),
        name="product",
    )(wm, vm, v, w)


def exchange_kernel(t, out, half, total, got, half_send, half_recv, send_sem, recv_sem):
    x, y, zh, zl, core = where_am_i()
    z = zh * 16 + zl
    chip = x * 4 + y
    bar = pltpu.get_barrier_semaphore()

    def greet(k, carry):
        chip2 = (chip + k) % 16
        pl.semaphore_signal(bar, inc=1, device_id=device(chip2 // 4, chip2 % 4, z, core), device_id_type=MESH)
        return carry
    lax.fori_loop(1, 16, greet, 0)
    partner = device(x, y, z, 1 - core)
    pl.semaphore_signal(bar, inc=1, device_id=partner, device_id_type=MESH)
    pl.semaphore_wait(bar, 16)

    swap = pltpu.make_async_remote_copy(
        t.at[:, :, 1 - core], half, half_send, half_recv, device_id=partner, device_id_type=MESH)
    swap.start()
    swap.wait_recv()
    total[...] = t[:, :, core] + half[...]

    def copy(k):
        chip2 = (chip + k) % 16
        return pltpu.make_async_remote_copy(
            total.at[chip2 % 4, chip2 // 4], got.at[chip], send_sem.at[k], recv_sem.at[chip],
            device_id=device(chip2 // 4, chip2 % 4, z, core), device_id_type=MESH)

    def start(k, carry):
        copy(k).start()
        return carry
    lax.fori_loop(1, 16, start, 0)
    own = pltpu.make_async_copy(total.at[y, x], got.at[chip], recv_sem.at[chip])
    own.start()
    own.wait()
    swap.wait_send()

    def finish(k, carry):
        chip2 = (chip + k) % 16
        pltpu.make_async_copy(got.at[chip2], got.at[chip2], recv_sem.at[chip2]).wait()
        copy(k).wait_send()
        return carry
    lax.fori_loop(1, 16, finish, 0)

    lane = lax.broadcasted_iota(jnp.int32, (8, 128), 1) // 32
    for xs in range(4):
        for b in range(4):
            part = [got[xs * 4 + ys, :, b * 128:(b + 1) * 128] for ys in range(4)]
            for mid in range(4):
                acc = None
                for ys in range(4):
                    turn = ((ys - mid) * 32) % 128
                    piece = pltpu.roll(part[ys], turn, axis=1) if turn else part[ys]
                    acc = piece if acc is None else jnp.where(lane == ys, piece, acc)
                out[16 * ((xs - b) % 4) + 4 * mid + b] = 0.5 * acc


def exchange(t):
    dma = pltpu.SemaphoreType.DMA
    vmem = pl.BlockSpec(memory_space=pltpu.VMEM)
    f32 = jnp.float32
    return pl.pallas_call(
        exchange_kernel,
        out_shape=jax.ShapeDtypeStruct((64, 8, 128), f32),
        in_specs=[vmem],
        out_specs=vmem,
        scratch_shapes=[
            pltpu.VMEM((4, 4, 8, 512), f32), pltpu.VMEM((4, 4, 8, 512), f32), pltpu.VMEM((16, 8, 512), f32),
            dma, dma, dma((16,)), dma((16,)),
        ],
        compiler_params=pltpu.CompilerParams(
            collective_id=1, has_side_effects=True, vmem_limit_bytes=16 * 2**20),
        name="exchange",
    )(t)


def shards(x_blocks, x_cols, q_blocks, q_cols):
    xb = x_blocks.reshape(3, 4, 2, 16, 128)
    qb = q_blocks.reshape(3, 4, 2, 16, 128)
    meta = jnp.pad(jnp.stack([x_cols, q_cols[0]]), ((0, 0), (0, 125))).reshape(2, 1, 128)
    w, wm, v, vm = gather(xb, qb, meta)
    t = product(
        wm.reshape(NZ * 8, 128), vm.reshape(64, 128),
        v.reshape(65 * 3, 4, 16, 128), w.reshape((NZ + 1) * 24, 2, 16, 128))
    return exchange(t.reshape(4, 4, 2, 8, 512))[None]


def solution(mesh):
    placed = (
        P(("row", "col"), None, None),
        P(("row", "col")),
        P("col", "row", None, None),
        P("col", "row"),
    )
    return jax.shard_map(
        shards, mesh=mesh, in_specs=placed, out_specs=P("col", None, "row", None), check_vma=False
    )
```

```python
import jax
import jax.numpy as jnp
from jax import lax
from jax.experimental import pallas as pl
from jax.experimental.pallas import tpu as pltpu
from jax.sharding import PartitionSpec as P

MESH = pl.DeviceIdType.MESH
NZ = 32
STEPS = 16
PARTS = 4
WIN = 132
GROUP = 33


def where_am_i():
    row, col = lax.axis_index("row"), lax.axis_index("col")
    x, zh, core = row // 4, (row // 2) % 2, row % 2
    zl, y = col // 4, col % 4
    return x, y, zh, zl, core


def device(x, y, z, core):
    return (x * 4 + (z // 16) * 2 + core, (z % 16) * 4 + y)


def gather_kernel(xb, qb, meta, w, wm, v, vm, w_send, w_recv, v_send, v_recv, ring_send, ring_recv):
    x, y, zh, zl, core = where_am_i()
    z = zh * 16 + zl
    a = zl // 4
    me = device(x, y, z, core)
    chip = x * 4 + y
    right = device(x, y, (z + 1) % NZ, core)
    left = device(x, y, (z + NZ - 1) % NZ, core)

    def is_me(dev):
        return (dev[0] == me[0]) & (dev[1] == me[1])

    bar = pltpu.get_barrier_semaphore()

    def greet(k, carry):
        chip2 = (chip + k // 2) % 16
        core2 = (core + k % 2) % 2
        pl.semaphore_signal(bar, inc=1, device_id=device(chip2 // 4, chip2 % 4, z, core2), device_id_type=MESH)
        return carry
    lax.fori_loop(1, 32, greet, 0)
    for dev in (right, left):
        pl.semaphore_signal(bar, inc=1, device_id=dev, device_id_type=MESH)
    pl.semaphore_wait(bar, 33)

    sent = []

    def send(src, dst, ssem, rsem, dev):
        mine = is_me(dev)
        copy = pltpu.make_async_remote_copy(src, dst, ssem, rsem, device_id=dev, device_id_type=MESH)

        @pl.when(jnp.logical_not(mine))
        def _():
            copy.start()

        @pl.when(mine)
        def _():
            pltpu.make_async_copy(src, dst, rsem).start()
        sent.append((mine, copy))

    for s in range(4):
        x_to = device((x + a) % 4, s, z, 0)
        send(xb.at[:, s], w.at[z, core * 4 + y], w_send.at[0, s, 0], w_recv.at[0], x_to)
        send(meta.at[0], wm.at[z, core * 4 + y], w_send.at[0, s, 1], w_recv.at[1], x_to)
        q_to = device((y + a) % 4, s, z, 1)
        send(qb.at[:, s], w.at[z, x * 2 + core], w_send.at[1, s, 0], w_recv.at[0], q_to)
        send(meta.at[1], wm.at[z, x * 2 + core], w_send.at[1, s, 1], w_recv.at[1], q_to)

    w[NZ] = jnp.zeros(w.shape[1:], w.dtype)
    v[64] = jnp.zeros(v.shape[1:], v.dtype)

    size = 8 // PARTS

    def chunk(plane, part):
        return wm.at[plane] if part == PARTS else w.at[plane, pl.ds(part * size, size)]

    def ring(way, step, part):
        ref = chunk((z + NZ - step) % NZ if way == 0 else (z + step) % NZ, part)
        return pltpu.make_async_remote_copy(
            ref, ref, ring_send.at[way, step, part], ring_recv.at[way, step, part],
            device_id=right if way == 0 else left, device_id_type=MESH)

    def arrived(way, step, part):
        ref = chunk((z + NZ - step - 1) % NZ if way == 0 else (z + step + 1) % NZ, part)
        pltpu.make_async_copy(ref, ref, ring_recv.at[way, step, part]).wait()

    own = (x + 4 - a) % 4

    def pass_on(plane):
        half, quarter, place = plane // 16, (plane % 16) // 4, plane % 4

        @pl.when((core == 0) & (half == (zl // 2) % 2) & (quarter == own))
        def _():
            def one(k, carry):
                chip2 = (chip + k) % 16
                to = device(chip2 // 4, chip2 % 4, z, 1)
                g = quarter * 16 + place * 4
                mine = pl.ds(zl % 2 * 4, 4)
                pltpu.make_async_remote_copy(
                    w.at[plane, mine, :, zh], v.at[pl.ds(g, 4), :, y], v_send.at[0], v_recv.at[0],
                    device_id=to, device_id_type=MESH).start()

                @pl.when(chip2 % 4 == y)
                def _():
                    pltpu.make_async_remote_copy(
                        wm.at[plane, mine], vm.at[pl.ds(g, 4)], v_send.at[1], v_recv.at[1],
                        device_id=to, device_id_type=MESH).start()
                return carry
            lax.fori_loop(0, 16, one, 0)

        @pl.when((core == 1) & (plane % 16 == zl))
        def _():
            def one(k, carry):
                chip2 = (chip + k) % 16
                to = device(chip2 // 4, chip2 % 4, z, 0)
                g = own * 16 + half * 8
                pltpu.make_async_remote_copy(
                    w.at[plane, :, :, zh], v.at[pl.ds(g, 8), :, y], v_send.at[0], v_recv.at[0],
                    device_id=to, device_id_type=MESH).start()

                @pl.when(chip2 % 4 == y)
                def _():
                    pltpu.make_async_remote_copy(
                        wm.at[plane], vm.at[pl.ds(g, 8)], v_send.at[1], v_recv.at[1],
                        device_id=to, device_id_type=MESH).start()
                return carry
            lax.fori_loop(0, 16, one, 0)

    pltpu.make_async_copy(w.at[z], w.at[z], w_recv.at[0]).wait()
    pltpu.make_async_copy(wm.at[z], wm.at[z], w_recv.at[1]).wait()
    for part in range(PARTS + 1):
        for way in range(2):
            ring(way, 0, part).start()
    pass_on(z)

    def ring_step(step, carry):
        for part in range(PARTS + 1):
            for way in range(2):
                arrived(way, step - 1, part)
                ring(way, step, part).start()
        pass_on((z + NZ - step) % NZ)
        pass_on((z + step) % NZ)
        return carry
    last = STEPS - 1
    lax.fori_loop(1, last, ring_step, 0)
    ends = [(0 if part < PARTS // 2 else 1, part) for part in range(PARTS + 1)]
    for way, part in ends:
        arrived(way, last - 1, part)
        ring(way, last, part).start()
    for way, part in ends:
        arrived(1 - way, last - 1, part)
    pass_on((z + NZ - last) % NZ)
    pass_on((z + last) % NZ)
    for way, part in ends:
        arrived(way, last, part)
    pass_on((z + 16) % NZ)

    for mine, copy in sent:
        @pl.when(jnp.logical_not(mine))
        def _():
            copy.wait_send()

    def ring_sent(step, carry):
        for part in range(PARTS + 1):
            for way in range(2):
                ring(way, step, part).wait_send()
        return carry
    lax.fori_loop(0, last, ring_sent, 0)
    for way, part in ends:
        ring(way, last, part).wait_send()
    rows = v.at[pl.ds(0, 64)]
    for n, ref in enumerate((rows, vm)):
        pltpu.make_async_copy(ref, ref, v_recv.at[n]).wait()
        pltpu.make_async_copy(ref, ref, v_send.at[n]).wait()


def gather(xb, qb, meta):
    bf, i32 = jnp.bfloat16, jnp.int32
    dma = pltpu.SemaphoreType.DMA
    vmem = pl.BlockSpec(memory_space=pltpu.VMEM)
    hbm = pl.BlockSpec(memory_space=pltpu.HBM)
    return pl.pallas_call(
        gather_kernel,
        out_shape=(
            jax.ShapeDtypeStruct((NZ + 1, 8, 3, 2, 16, 128), bf),
            jax.ShapeDtypeStruct((NZ, 8, 1, 128), i32),
            jax.ShapeDtypeStruct((65, 3, 4, 16, 128), bf),
            jax.ShapeDtypeStruct((64, 1, 128), i32),
        ),
        in_specs=[hbm, hbm, vmem],
        out_specs=(vmem,) * 4,
        scratch_shapes=[
            dma((2, 4, 2)), dma((2,)), dma((2,)), dma((2,)),
            dma((2, STEPS, PARTS + 1)), dma((2, STEPS, PARTS + 1)),
        ],
        compiler_params=pltpu.CompilerParams(
            collective_id=0, has_side_effects=True, vmem_limit_bytes=40 * 2**20),
        name="gather",
    )(xb, qb, meta)


def tables_kernel(wm, vm, rows):
    x, y, zh, zl, core = where_am_i()
    v_cols, w_cols = vm[...], wm[...]
    first = v_cols[0:1, 0:1]
    row = lax.broadcasted_iota(jnp.int32, (64, 128), 0) // 16
    lane = lax.broadcasted_iota(jnp.int32, (64, 128), 1)
    off = ((v_cols - first + 4096) & 8191) - 4096 - row
    off = jnp.where(lane < 3, off, 8192).astype(jnp.float32)
    least = jnp.min(jnp.min(off, axis=1, keepdims=True), axis=0, keepdims=True)
    base = first + least.astype(jnp.int32)

    def hits(cols, none):
        n = cols.shape[0]
        place = lax.broadcasted_iota(jnp.int32, (n, 256), 1)
        ids = (lax.broadcasted_iota(jnp.int32, (n, 256), 0) * 3 - none).astype(jnp.float32)
        total = jnp.zeros((n, 256), jnp.float32)
        for k in range(3):
            total += jnp.where(((cols[:, k:k + 1] - base) & 8191) == place, ids + k, 0.0)
        return total

    none_v, none_w = 192, NZ * 24
    in_v = jnp.sum(hits(v_cols, none_v).reshape(4, 16, 256), axis=1)
    in_w = hits(w_cols, none_w).reshape(2, 4, 4, 8, 256)
    from_q = jnp.sum(jnp.sum(in_w, axis=0), axis=2)
    over_place = in_w[:, :, 0] + in_w[:, :, 1] + in_w[:, :, 2] + in_w[:, :, 3]
    of_core = lax.broadcasted_iota(jnp.int32, (2, 4, 8, 256), 2) // 4
    from_x = [jnp.sum(jnp.where(of_core == n, over_place, 0.0), axis=2) for n in range(2)]
    for b in range(4):
        for mid in range(4):
            of_x = from_x[mid % 2][mid // 2, b:b + 1]
            of_q = from_q[(3 - b) % 4, mid:mid + 1]
            for xs in range(3):
                of_q = jnp.where(x == xs, from_q[(xs - b) % 4, mid:mid + 1], of_q)
            m = b * 4 + mid
            rows[m:m + 1] = jnp.where(core == 0, of_x, of_q).astype(jnp.int32) + none_w
    rows[16:20] = in_v.astype(jnp.int32) + none_v
    rows[20:24] = jnp.zeros((4, 256), jnp.int32)


def tables(wm, vm):
    vmem = pl.BlockSpec(memory_space=pltpu.VMEM)
    return pl.pallas_call(
        tables_kernel,
        out_shape=jax.ShapeDtypeStruct((24, 256), jnp.int32),
        in_specs=[vmem] * 2,
        out_specs=vmem,
        name="tables",
    )(wm, vm)


def product_kernel(tab, v, w, out, t, half, total, got, half_send, half_recv, send_sem, recv_sem):
    x, y, zh, zl, core = where_am_i()
    z = zh * 16 + zl
    chip = x * 4 + y
    bar = pltpu.get_barrier_semaphore()

    def greet(k, carry):
        chip2 = (chip + k) % 16
        pl.semaphore_signal(bar, inc=1, device_id=device(chip2 // 4, chip2 % 4, z, core), device_id_type=MESH)
        return carry
    lax.fori_loop(1, 16, greet, 0)
    partner = device(x, y, z, 1 - core)
    pl.semaphore_signal(bar, inc=1, device_id=partner, device_id_type=MESH)

    def multiply(n, first, last):
        def step(g, carry):
            vs, ws = [], []
            for u in range(GROUP):
                at = g * GROUP + u
                vs.append(jnp.concatenate([v[tab[16 + c, at]].reshape(64, 128) for c in range(4)], axis=0))
                ws.append(jnp.concatenate([w[tab[n * 8 + m, at]].reshape(32, 128) for m in range(8)], axis=0))
            left = jnp.concatenate(vs, axis=1)
            right = jnp.concatenate(ws, axis=1)
            more = lax.dot_general(left, right, (((1,), (1,)), ((), ())), preferred_element_type=jnp.float32)
            t[n] += more.reshape(4, 4, 2, 8, 256)
            return carry
        lax.fori_loop(first, last, step, 0)

    def swap(n, c):
        return pltpu.make_async_remote_copy(
            t.at[n, c, :, 1 - core], half.at[n, c], half_send.at[n, c], half_recv.at[n, c],
            device_id=partner, device_id_type=MESH)

    def copy(n, c, px):
        return pltpu.make_async_remote_copy(
            total.at[n, c, px], got.at[n, chip], send_sem.at[n, c, px], recv_sem.at[n, chip],
            device_id=device(px, c, z, core), device_id_type=MESH)

    order = [(y + k) % 4 for k in (2, 1, 3, 0)]

    def swap_all(n):
        for c in order:
            swap(n, c).start()

    def send_all(n):
        for k, c in enumerate(order):
            swap(n, c).wait_recv()
            total[n, c] = t[n, c, :, core] + half[n, c]
            for k2 in (2, 1, 3):
                copy(n, c, (x + k2) % 4).start()
            if k < 3:
                copy(n, c, x).start()
            else:
                pltpu.make_async_copy(total.at[n, c, x], got.at[n, chip], recv_sem.at[n, chip]).start()

    lane = lax.broadcasted_iota(jnp.int32, (8, 128), 1) // 32

    def put_together(n):
        for xs in range(4):
            for ys in range(4):
                chip2 = xs * 4 + ys
                pltpu.make_async_copy(got.at[n, chip2], got.at[n, chip2], recv_sem.at[n, chip2]).wait()
            for b2 in range(2):
                b = n * 2 + b2
                part = [got[n, xs * 4 + ys, :, b2 * 128:(b2 + 1) * 128] for ys in range(4)]
                for mid in range(4):
                    acc = None
                    for ys in range(4):
                        turn = ((ys - mid) * 32) % 128
                        piece = pltpu.roll(part[ys], turn, axis=1) if turn else part[ys]
                        acc = piece if acc is None else jnp.where(lane == ys, piece, acc)
                    out[16 * ((xs - b) % 4) + 4 * mid + b] = 0.5 * acc

    steps = WIN // GROUP
    t[...] = jnp.zeros_like(t)
    multiply(0, 0, steps)
    pl.semaphore_wait(bar, 16)
    swap_all(0)
    multiply(1, 0, 2)
    send_all(0)
    multiply(1, 2, steps)
    swap_all(1)
    send_all(1)
    put_together(0)
    put_together(1)
    for n in range(2):
        for k, c in enumerate(order):
            swap(n, c).wait_send()
            for k2 in (2, 1, 3):
                copy(n, c, (x + k2) % 4).wait_send()
            if k < 3:
                copy(n, c, x).wait_send()


def product(tab, v, w):
    dma = pltpu.SemaphoreType.DMA
    vmem = pl.BlockSpec(memory_space=pltpu.VMEM)
    smem = pl.BlockSpec(memory_space=pltpu.SMEM)
    f32 = jnp.float32
    return pl.pallas_call(
        product_kernel,
        out_shape=jax.ShapeDtypeStruct((64, 8, 128), f32),
        in_specs=[smem, vmem, vmem],
        out_specs=vmem,
        scratch_shapes=[
            pltpu.VMEM((2, 4, 4, 2, 8, 256), f32), pltpu.VMEM((2, 4, 4, 8, 256), f32),
            pltpu.VMEM((2, 4, 4, 8, 256), f32), pltpu.VMEM((2, 16, 8, 256), f32),
            dma((2, 4)), dma((2, 4)), dma((2, 4, 4)), dma((2, 16)),
        ],
        compiler_params=pltpu.CompilerParams(
            collective_id=1, has_side_effects=True, vmem_limit_bytes=40 * 2**20),
        name="product",
    )(tab, v, w)


def shards(x_blocks, x_cols, q_blocks, q_cols):
    xb = x_blocks.reshape(3, 4, 2, 16, 128)
    qb = q_blocks.reshape(3, 4, 2, 16, 128)
    meta = jnp.pad(jnp.stack([x_cols, q_cols[0]]), ((0, 0), (0, 125))).reshape(2, 1, 128)
    w, wm, v, vm = gather(xb, qb, meta)
    out = product(
        tables(wm.reshape(NZ * 8, 128), vm.reshape(64, 128)),
        v.reshape(65 * 3, 4, 16, 128), w.reshape((NZ + 1) * 24, 2, 16, 128))
    return out[None]


def solution(mesh):
    placed = (
        P(("row", "col"), None, None),
        P(("row", "col")),
        P("col", "row", None, None),
        P("col", "row"),
    )
    return jax.shard_map(
        shards, mesh=mesh, in_specs=placed, out_specs=P("col", None, "row", None), check_vma=False
    )
```

```python
import jax
import jax.numpy as jnp
from jax import lax
from jax.experimental import pallas as pl
from jax.experimental.pallas import tpu as pltpu
from jax.sharding import PartitionSpec as P

MESH = pl.DeviceIdType.MESH
NZ = 32
STEPS = 16
PARTS = 4
WIN = 132
GROUP = 33


def where_am_i():
    row, col = lax.axis_index("row"), lax.axis_index("col")
    x, zh, core = row // 4, (row // 2) % 2, row % 2
    zl, y = col // 4, col % 4
    return x, y, zh, zl, core


def device(x, y, z, core):
    return (x * 4 + (z // 16) * 2 + core, (z % 16) * 4 + y)


def near(n):
    return n + n // 2 * (5 - 2 * n)


def gather_kernel(xb, qb, meta, w, wm, v, vm, w_send, w_recv, v_send, v_recv, ring_send, ring_recv):
    x, y, zh, zl, core = where_am_i()
    z = zh * 16 + zl
    a = zl // 4
    me = device(x, y, z, core)
    chip = x * 4 + y
    right = device(x, y, (z + 1) % NZ, core)
    left = device(x, y, (z + NZ - 1) % NZ, core)

    def is_me(dev):
        return (dev[0] == me[0]) & (dev[1] == me[1])

    bar = pltpu.get_barrier_semaphore()

    def greet(k, carry):
        chip2 = (chip + k // 2) % 16
        core2 = (core + k % 2) % 2
        pl.semaphore_signal(bar, inc=1, device_id=device(chip2 // 4, chip2 % 4, z, core2), device_id_type=MESH)
        return carry
    lax.fori_loop(1, 32, greet, 0)
    for dev in (right, left):
        pl.semaphore_signal(bar, inc=1, device_id=dev, device_id_type=MESH)
    pl.semaphore_wait(bar, 33)

    sent = []

    def send(src, dst, ssem, rsem, dev):
        mine = is_me(dev)
        copy = pltpu.make_async_remote_copy(src, dst, ssem, rsem, device_id=dev, device_id_type=MESH)

        @pl.when(jnp.logical_not(mine))
        def _():
            copy.start()

        @pl.when(mine)
        def _():
            pltpu.make_async_copy(src, dst, rsem).start()
        sent.append((mine, copy))

    for s in range(4):
        x_to = device((x + a) % 4, s, z, 0)
        send(xb.at[:, s], w.at[z, core * 4 + y], w_send.at[0, s, 0], w_recv.at[0], x_to)
        send(meta.at[0], wm.at[z, core * 4 + y], w_send.at[0, s, 1], w_recv.at[1], x_to)
        q_to = device((y + a) % 4, s, z, 1)
        send(qb.at[:, s], w.at[z, x * 2 + core], w_send.at[1, s, 0], w_recv.at[0], q_to)
        send(meta.at[1], wm.at[z, x * 2 + core], w_send.at[1, s, 1], w_recv.at[1], q_to)

    w[NZ] = jnp.zeros(w.shape[1:], w.dtype)
    v[64] = jnp.zeros(v.shape[1:], v.dtype)

    size = 8 // PARTS

    def chunk(plane, part):
        return wm.at[plane] if part == PARTS else w.at[plane, pl.ds(part * size, size)]

    def ring(way, step, part):
        ref = chunk((z + NZ - step) % NZ if way == 0 else (z + step) % NZ, part)
        return pltpu.make_async_remote_copy(
            ref, ref, ring_send.at[way, step, part], ring_recv.at[way, step, part],
            device_id=right if way == 0 else left, device_id_type=MESH)

    def arrived(way, step, part):
        ref = chunk((z + NZ - step - 1) % NZ if way == 0 else (z + step + 1) % NZ, part)
        pltpu.make_async_copy(ref, ref, ring_recv.at[way, step, part]).wait()

    own = (x + 4 - a) % 4

    def pass_on(plane):
        half, quarter, place = plane // 16, (plane % 16) // 4, plane % 4

        @pl.when((core == 0) & (half == (zl // 2) % 2) & (quarter == own))
        def _():
            def one(k, carry):
                px, py = (x + near(k // 4)) % 4, (y + near(k % 4)) % 4
                to = device(px, py, z, 1)
                g = quarter * 16 + place * 4
                mine = pl.ds(zl % 2 * 4, 4)
                pltpu.make_async_remote_copy(
                    w.at[plane, mine, :, zh], v.at[pl.ds(g, 4), :, y], v_send.at[0], v_recv.at[0],
                    device_id=to, device_id_type=MESH).start()

                @pl.when(py == y)
                def _():
                    pltpu.make_async_remote_copy(
                        wm.at[plane, mine], vm.at[pl.ds(g, 4)], v_send.at[1], v_recv.at[1],
                        device_id=to, device_id_type=MESH).start()
                return carry
            lax.fori_loop(0, 16, one, 0)

        @pl.when((core == 1) & (plane % 16 == zl))
        def _():
            def one(k, carry):
                px, py = (x + near(k // 4)) % 4, (y + near(k % 4)) % 4
                to = device(px, py, z, 0)
                g = own * 16 + half * 8
                pltpu.make_async_remote_copy(
                    w.at[plane, :, :, zh], v.at[pl.ds(g, 8), :, y], v_send.at[0], v_recv.at[0],
                    device_id=to, device_id_type=MESH).start()

                @pl.when(py == y)
                def _():
                    pltpu.make_async_remote_copy(
                        wm.at[plane], vm.at[pl.ds(g, 8)], v_send.at[1], v_recv.at[1],
                        device_id=to, device_id_type=MESH).start()
                return carry
            lax.fori_loop(0, 16, one, 0)

    pltpu.make_async_copy(w.at[z], w.at[z], w_recv.at[0]).wait()
    pltpu.make_async_copy(wm.at[z], wm.at[z], w_recv.at[1]).wait()
    for part in range(PARTS + 1):
        for way in range(2):
            ring(way, 0, part).start()
    pass_on(z)

    def ring_step(step, carry):
        for part in range(PARTS + 1):
            for way in range(2):
                arrived(way, step - 1, part)
                ring(way, step, part).start()
        pass_on((z + NZ - step) % NZ)
        pass_on((z + step) % NZ)
        return carry
    last = STEPS - 1
    lax.fori_loop(1, last, ring_step, 0)
    ends = [(0 if part < PARTS // 2 else 1, part) for part in range(PARTS + 1)]
    for way, part in ends:
        arrived(way, last - 1, part)
        ring(way, last, part).start()
    for way, part in ends:
        arrived(1 - way, last - 1, part)
    pass_on((z + NZ - last) % NZ)
    pass_on((z + last) % NZ)
    for way, part in ends:
        arrived(way, last, part)
    pass_on((z + 16) % NZ)

    for mine, copy in sent:
        @pl.when(jnp.logical_not(mine))
        def _():
            copy.wait_send()

    def ring_sent(step, carry):
        for part in range(PARTS + 1):
            for way in range(2):
                ring(way, step, part).wait_send()
        return carry
    lax.fori_loop(0, last, ring_sent, 0)
    for way, part in ends:
        ring(way, last, part).wait_send()
    rows = v.at[pl.ds(0, 64)]
    for n, ref in enumerate((rows, vm)):
        pltpu.make_async_copy(ref, ref, v_recv.at[n]).wait()
        pltpu.make_async_copy(ref, ref, v_send.at[n]).wait()


def gather(xb, qb, meta):
    bf, i32 = jnp.bfloat16, jnp.int32
    dma = pltpu.SemaphoreType.DMA
    vmem = pl.BlockSpec(memory_space=pltpu.VMEM)
    hbm = pl.BlockSpec(memory_space=pltpu.HBM)
    return pl.pallas_call(
        gather_kernel,
        out_shape=(
            jax.ShapeDtypeStruct((NZ + 1, 8, 3, 2, 16, 128), bf),
            jax.ShapeDtypeStruct((NZ, 8, 1, 128), i32),
            jax.ShapeDtypeStruct((65, 3, 4, 16, 128), bf),
            jax.ShapeDtypeStruct((64, 1, 128), i32),
        ),
        in_specs=[hbm, hbm, vmem],
        out_specs=(vmem,) * 4,
        scratch_shapes=[
            dma((2, 4, 2)), dma((2,)), dma((2,)), dma((2,)),
            dma((2, STEPS, PARTS + 1)), dma((2, STEPS, PARTS + 1)),
        ],
        compiler_params=pltpu.CompilerParams(
            collective_id=0, has_side_effects=True, vmem_limit_bytes=40 * 2**20),
        name="gather",
    )(xb, qb, meta)


def product_kernel(wm, vm, v, w, out, rows, tab, tab_sem):
    x, y, zh, zl, core = where_am_i()

    v_cols, w_cols = vm[...], wm[...]
    first = v_cols[0:1, 0:1]
    row = lax.broadcasted_iota(jnp.int32, (64, 128), 0) // 16
    lane = lax.broadcasted_iota(jnp.int32, (64, 128), 1)
    off = ((v_cols - first + 4096) & 8191) - 4096 - row
    off = jnp.where(lane < 3, off, 8192).astype(jnp.float32)
    least = jnp.min(jnp.min(off, axis=1, keepdims=True), axis=0, keepdims=True)
    base = first + least.astype(jnp.int32)

    def hits(cols, none):
        n = cols.shape[0]
        place = lax.broadcasted_iota(jnp.int32, (n, 256), 1)
        ids = (lax.broadcasted_iota(jnp.int32, (n, 256), 0) * 3 - none).astype(jnp.float32)
        total = jnp.zeros((n, 256), jnp.float32)
        for k in range(3):
            total += jnp.where(((cols[:, k:k + 1] - base) & 8191) == place, ids + k, 0.0)
        return total

    none_v, none_w = 192, NZ * 24
    in_v = jnp.sum(hits(v_cols, none_v).reshape(4, 16, 256), axis=1)
    in_w = hits(w_cols, none_w).reshape(2, 4, 4, 8, 256)
    from_q = jnp.sum(jnp.sum(in_w, axis=0), axis=2)
    over_place = in_w[:, :, 0] + in_w[:, :, 1] + in_w[:, :, 2] + in_w[:, :, 3]
    of_core = lax.broadcasted_iota(jnp.int32, (2, 4, 8, 256), 2) // 4
    from_x = [jnp.sum(jnp.where(of_core == n, over_place, 0.0), axis=2) for n in range(2)]
    for b in range(4):
        for mid in range(4):
            of_x = from_x[mid % 2][mid // 2, b:b + 1]
            of_q = from_q[(3 - b) % 4, mid:mid + 1]
            for xs in range(3):
                of_q = jnp.where(x == xs, from_q[(xs - b) % 4, mid:mid + 1], of_q)
            m = b * 4 + mid
            rows[m:m + 1] = jnp.where(core == 0, of_x, of_q).astype(jnp.int32) + none_w
    rows[16:20] = in_v.astype(jnp.int32) + none_v
    tab_in = pltpu.make_async_copy(rows, tab, tab_sem)
    tab_in.start()
    out[...] = jnp.zeros_like(out)
    tab_in.wait()

    def step(g, carry):
        vs, ws = [], []
        for u in range(GROUP):
            at = g * GROUP + u
            vs.append(jnp.concatenate([v[tab[16 + c, at]].reshape(64, 128) for c in range(4)], axis=0))
            ws.append(jnp.concatenate([w[tab[m, at]].reshape(32, 128) for m in range(16)], axis=0))
        left = jnp.concatenate(vs, axis=1)
        right = jnp.concatenate(ws, axis=1)
        out[...] += lax.dot_general(left, right, (((1,), (1,)), ((), ())), preferred_element_type=jnp.float32)
        return carry
    lax.fori_loop(0, WIN // GROUP, step, 0)


def product(wm, vm, v, w):
    vmem = pl.BlockSpec(memory_space=pltpu.VMEM)
    return pl.pallas_call(
        product_kernel,
        out_shape=jax.ShapeDtypeStruct((256, 512), jnp.float32),
        in_specs=[vmem] * 4,
        out_specs=vmem,
        scratch_shapes=[
            pltpu.VMEM((24, 256), jnp.int32), pltpu.SMEM((24, 256), jnp.int32),
            pltpu.SemaphoreType.DMA,
        ],
        compiler_params=pltpu.CompilerParams(vmem_limit_bytes=40 * 2**20),
        name="product",
    )(wm, vm, v, w)


def exchange_kernel(t, out, half, total, got, half_send, half_recv, send_sem, recv_sem):
    x, y, zh, zl, core = where_am_i()
    z = zh * 16 + zl
    chip = x * 4 + y
    bar = pltpu.get_barrier_semaphore()

    def greet(k, carry):
        chip2 = (chip + k) % 16
        pl.semaphore_signal(bar, inc=1, device_id=device(chip2 // 4, chip2 % 4, z, core), device_id_type=MESH)
        return carry
    lax.fori_loop(1, 16, greet, 0)
    partner = device(x, y, z, 1 - core)
    pl.semaphore_signal(bar, inc=1, device_id=partner, device_id_type=MESH)
    pl.semaphore_wait(bar, 16)

    def swap(c):
        return pltpu.make_async_remote_copy(
            t.at[c, :, 1 - core], half.at[c], half_send.at[c], half_recv.at[c],
            device_id=partner, device_id_type=MESH)

    def copy(c, px):
        return pltpu.make_async_remote_copy(
            total.at[c, px], got.at[chip], send_sem.at[c, px], recv_sem.at[chip],
            device_id=device(px, c, z, core), device_id_type=MESH)

    order = [(y + k) % 4 for k in (2, 1, 3, 0)]
    for c in order:
        swap(c).start()
    for n, c in enumerate(order):
        swap(c).wait_recv()
        total[c] = t[c, :, core] + half[c]
        for k in (2, 1, 3):
            copy(c, (x + k) % 4).start()
        if n < 3:
            copy(c, x).start()
        else:
            pltpu.make_async_copy(total.at[c, x], got.at[chip], recv_sem.at[chip]).start()

    lane = lax.broadcasted_iota(jnp.int32, (8, 128), 1) // 32
    for xs in range(4):
        for ys in range(4):
            chip2 = xs * 4 + ys
            pltpu.make_async_copy(got.at[chip2], got.at[chip2], recv_sem.at[chip2]).wait()
        for b in range(4):
            part = [got[xs * 4 + ys, :, b * 128:(b + 1) * 128] for ys in range(4)]
            for mid in range(4):
                acc = None
                for ys in range(4):
                    turn = ((ys - mid) * 32) % 128
                    piece = pltpu.roll(part[ys], turn, axis=1) if turn else part[ys]
                    acc = piece if acc is None else jnp.where(lane == ys, piece, acc)
                out[16 * ((xs - b) % 4) + 4 * mid + b] = 0.5 * acc
    for n, c in enumerate(order):
        swap(c).wait_send()
        for k in (2, 1, 3):
            copy(c, (x + k) % 4).wait_send()
        if n < 3:
            copy(c, x).wait_send()


def exchange(t):
    dma = pltpu.SemaphoreType.DMA
    vmem = pl.BlockSpec(memory_space=pltpu.VMEM)
    f32 = jnp.float32
    return pl.pallas_call(
        exchange_kernel,
        out_shape=jax.ShapeDtypeStruct((64, 8, 128), f32),
        in_specs=[vmem],
        out_specs=vmem,
        scratch_shapes=[
            pltpu.VMEM((4, 4, 8, 512), f32), pltpu.VMEM((4, 4, 8, 512), f32), pltpu.VMEM((16, 8, 512), f32),
            dma((4,)), dma((4,)), dma((4, 4)), dma((16,)),
        ],
        compiler_params=pltpu.CompilerParams(
            collective_id=1, has_side_effects=True, vmem_limit_bytes=16 * 2**20),
        name="exchange",
    )(t)


def shards(x_blocks, x_cols, q_blocks, q_cols):
    xb = x_blocks.reshape(3, 4, 2, 16, 128)
    qb = q_blocks.reshape(3, 4, 2, 16, 128)
    meta = jnp.pad(jnp.stack([x_cols, q_cols[0]]), ((0, 0), (0, 125))).reshape(2, 1, 128)
    w, wm, v, vm = gather(xb, qb, meta)
    t = product(
        wm.reshape(NZ * 8, 128), vm.reshape(64, 128),
        v.reshape(65 * 3, 4, 16, 128), w.reshape((NZ + 1) * 24, 2, 16, 128))
    return exchange(t.reshape(4, 4, 2, 8, 512))[None]


def solution(mesh):
    placed = (
        P(("row", "col"), None, None),
        P(("row", "col")),
        P("col", "row", None, None),
        P("col", "row"),
    )
    return jax.shard_map(
        shards, mesh=mesh, in_specs=placed, out_specs=P("col", None, "row", None), check_vma=False
    )
```
